32 devices in a mesh: clus: 4 (over y, x), leaf: 8 (over z, core).
Axes of the slice: x: 2, y: 2, z: 4, core: 2. Of those that a mesh axis runs over, the one named last changes fastest.
Arguments:
- points: bfloat16 [64, 65536], P(None, ('clus', 'leaf')), may hold values from -6 to 6
- weights: bfloat16 [512, 65536], P(None, ('clus', 'leaf')), may hold values from -2 to 2
- targets: bfloat16 [512, 65536], P(None, ('clus', 'leaf')), may hold values from -6 to 6
- near_lists: int32 [128, 4], P(('clus', 'leaf')), may hold values from 0 to 127, as said below
- tile_counts: int32 [128], P(('clus', 'leaf')), may hold values from 2 to 4, as said below
- skeleton: int32 [32, 256], P(('clus', 'leaf')), may hold values from 0 to 2047, as said below
Outputs:
- precond: float32 [512, 65536], P(None, ('clus', 'leaf'))
The draws below stay inside these ranges and needn't reach their ends.
Inputs may be any that keep to these rules, and one draw needn't show every extreme that they name: `near_lists`: row g lists cluster ids; its first entry is g; its first tile_counts[g] entries are distinct, and the rest repeat g. Every listed cluster lies on a device with the same leaf index as cluster g's device and a clus index at most 1 away; some cluster lists one exactly 1 away. `tile_counts`: some cluster has exactly 4 tiles. `skeleton`: each row holds 256 distinct indices of points of its device; their order matters.
All inputs are finite; a program needn't handle non-finite values.
Results may differ from the reference program's by a relative error of at most 0.0039.
Values may be sent and summed in bfloat16 or wider, within the bound.
A program may use at most 128 MiB of HBM per device.

```python
import jax
import jax.numpy as jnp
from jax import lax

FEATURES = 64
RHS_COLS = 512
CLUSTER_PTS = 512
SKELETON = 256
CLUS_DEV = 4
TILES_MAX = 4
NEAR_REACH = 1
PTS_DEV = 2048
CLUSTERS = 128
POINTS = 65536
LEVELS = 3
N_CLUS = 4
N_LEAF = 8
DEVICES = 32


def draw_points(key, part):
    base_key = jax.random.fold_in(key, 53)
    sign_key, center_key, latent_key, noise_key = jax.random.split(base_key, 4)
    sign_cols = jnp.where(jax.random.bernoulli(sign_key, 0.5, (FEATURES, 2)), 1.0, -1.0).astype(jnp.float32)
    centers = jax.random.uniform(center_key, (DEVICES, 2), jnp.float32, -0.75, 0.75)
    owner_dev = jnp.arange(POINTS, dtype=jnp.int32) // PTS_DEV
    centre_cols = jnp.take(centers, owner_dev, axis=0)
    latent = jax.random.uniform(latent_key, (POINTS, 2), jnp.float32, -1.0, 1.0)
    noise_part = 0.15 * jax.random.normal(noise_key, (FEATURES, POINTS), jnp.float32)
    coords = centre_cols + latent
    values = (sign_cols[:, 0:1] * coords[None, :, 0] + sign_cols[:, 1:2] * coords[None, :, 1]) * 0.70710678 + noise_part
    return jnp.clip(values, -6.0, 6.0).astype(jnp.bfloat16)


def near_tables(key):
    base_key = jax.random.fold_in(key, 31)
    score_key, count_key = jax.random.split(base_key)
    window_len = 2 * NEAR_REACH + 1
    choices_n = window_len * CLUS_DEV
    cluster_id = jnp.arange(CLUSTERS, dtype=jnp.int32)
    device_id = cluster_id // CLUS_DEV
    clus_idx = device_id // N_LEAF
    leaf_idx = device_id % N_LEAF
    slot_ids = jnp.arange(choices_n, dtype=jnp.int32)
    offsets = slot_ids // CLUS_DEV - NEAR_REACH
    member = slot_ids % CLUS_DEV
    cand_clus = clus_idx[:, None] + offsets[None, :]
    valid_cand = (cand_clus >= 0) & (cand_clus < N_CLUS)
    cand_id = (cand_clus * N_LEAF + leaf_idx[:, None]) * CLUS_DEV + member[None, :]
    own_cand = cand_id == cluster_id[:, None]
    scores = jax.random.randint(score_key, (CLUSTERS, choices_n), 0, 1 << 20, dtype=jnp.int32) * choices_n + slot_ids[None, :] + 1
    forced = (cluster_id[:, None] == 0) & (offsets[None, :] == NEAR_REACH) & (member[None, :] == 0)
    scores = jnp.where(forced, 0, scores)
    scores = jnp.where(own_cand, -1, scores)
    scores = jnp.where(valid_cand, scores, 1 << 30)
    order_idx = jnp.argsort(scores, axis=1, stable=True)
    ranked = jnp.take_along_axis(cand_id, order_idx, axis=1)[:, :TILES_MAX]
    draws_u = jax.random.randint(count_key, (CLUSTERS,), 0, 64, dtype=jnp.int32)
    counts = 2 + draws_u * draws_u * (TILES_MAX - 2) // 3969
    counts = jnp.where(cluster_id == 0, TILES_MAX, counts)
    slot_pos = jnp.arange(TILES_MAX, dtype=jnp.int32)[None, :]
    listed = jnp.where(slot_pos < counts[:, None], ranked, cluster_id[:, None])
    return (listed.astype(jnp.int32), counts.astype(jnp.int32))


def draw_near_lists(key, part):
    return near_tables(key)[0]


def draw_tile_counts(key, part):
    return near_tables(key)[1]


def draw_skeleton(key, part):

    def one_row(row_key):
        first_key, second_key = jax.random.split(row_key)
        inner = (jax.random.permutation(first_key, PTS_DEV - 2) + 1).astype(jnp.int32)
        chosen = jnp.concatenate([jnp.array([0, PTS_DEV - 1], dtype=jnp.int32), inner[:SKELETON - 2]])
        return chosen[jax.random.permutation(second_key, SKELETON)]
    row_keys = jax.random.split(jax.random.fold_in(key, 17), DEVICES)
    return jax.vmap(one_row)(row_keys).astype(jnp.int32)


def level_of(rng, extent, shards, low, top_value):
    def one(dim, blocks):
        heights = jax.random.uniform(jax.random.fold_in(jax.random.fold_in(rng, 6), dim), (blocks,), jnp.float32, low / len(shards), top_value / len(shards))
        return jnp.repeat(jnp.exp(heights), extent[dim] // blocks).reshape((-1,) + (1,) * (len(extent) - dim - 1))

    level = one(*shards[0])
    for cut in shards[1:]:
        level = level * one(*cut)
    return level


def bell_draw(key, dims, scale, most, pieces=(), held_as=jnp.bfloat16):
    values = jax.random.normal(key, dims, jnp.float32) * scale
    if len(pieces) > 0:
        values = level_of(key, dims, pieces, -0.22, 0.18) * values
    return jnp.clip(values, min=-most, max=most).astype(held_as)


def setup_inputs(seed: int = 0) -> dict:
    seeds = jax.random.split(jax.random.key(seed), 7)
    return {
        "points": draw_points(jax.random.fold_in(seeds[6], 71), 0),
        "weights": bell_draw(seeds[1], (RHS_COLS, POINTS), 0.15, 2.0, ((1, 32),)),
        "targets": bell_draw(seeds[2], (RHS_COLS, POINTS), 1.0, 6.0, ((1, 32),)),
        "near_lists": draw_near_lists(jax.random.fold_in(seeds[6], 71), 0),
        "tile_counts": draw_tile_counts(jax.random.fold_in(seeds[6], 71), 0),
        "skeleton": draw_skeleton(jax.random.fold_in(seeds[6], 71), 0),
    }


ridge_term = 0.5
node_shift = 4.0

def kernel_tile(row_pts, col_pts):
    row_pts = row_pts.astype(jnp.float32)
    col_pts = col_pts.astype(jnp.float32)
    cross_dot = lax.dot_general(row_pts.astype(jnp.float32), col_pts.astype(jnp.float32), (((0,), (0,)), ((), ())), precision=lax.Precision.HIGHEST, preferred_element_type=jnp.float32)
    row_sq = jnp.sum(row_pts * row_pts, axis=0)
    col_sq = jnp.sum(col_pts * col_pts, axis=0)
    scale_exp = 2.0 / row_pts.shape[0]
    return jnp.exp(-scale_exp * (row_sq[:, None] + col_sq[None, :] - 2.0 * cross_dot))

def solve_right(factor_low, values):
    partial_sol = lax.linalg.triangular_solve(factor_low, values, left_side=False, lower=True, transpose_a=True)
    return lax.linalg.triangular_solve(factor_low, partial_sol, left_side=False, lower=True, transpose_a=False)

def node_solve(node_pts, node_res):
    gram_mat = kernel_tile(node_pts, node_pts) + node_shift * jnp.eye(node_pts.shape[1], dtype=jnp.float32)
    return solve_right(jnp.linalg.cholesky(gram_mat), node_res)

def tile_term(own_pts, other_pts, other_w):
    tile_low = lax.optimization_barrier(kernel_tile(other_pts, own_pts).astype(jnp.bfloat16))
    return jnp.dot(other_w.astype(jnp.float32), tile_low.astype(jnp.float32), precision=lax.Precision.HIGHEST)

def near_field(points, weights, near_lists, tile_counts):

    def one_cluster(cluster_id):
        own_pts = lax.dynamic_slice_in_dim(points, (cluster_id * CLUSTER_PTS).astype(jnp.int32), CLUSTER_PTS, 1)

        def add_tile(slot_idx, summed):
            listed_id = near_lists[cluster_id, slot_idx]

            def compute():
                begin_col = (listed_id * CLUSTER_PTS).astype(jnp.int32)
                other_pts = lax.dynamic_slice_in_dim(points, begin_col, CLUSTER_PTS, 1)
                other_w = lax.dynamic_slice_in_dim(weights, begin_col, CLUSTER_PTS, 1)
                return tile_term(own_pts, other_pts, other_w)

            def nothing():
                return jnp.zeros((RHS_COLS, CLUSTER_PTS), jnp.float32)
            return summed + lax.cond(slot_idx < tile_counts[cluster_id], compute, nothing)
        return lax.fori_loop(0, TILES_MAX, add_tile, jnp.zeros((RHS_COLS, CLUSTER_PTS), jnp.float32))
    blocks = lax.map(one_cluster, jnp.arange(CLUSTERS, dtype=jnp.int32))
    return jnp.transpose(blocks, (1, 0, 2)).reshape(RHS_COLS, POINTS)

def tree_correction(points, residual, skeleton):
    row_idx = (jnp.arange(DEVICES, dtype=jnp.int32)[:, None] * PTS_DEV + skeleton).astype(jnp.int32)
    node_pts = jnp.transpose(jnp.take(points, row_idx, axis=1), (1, 0, 2))
    node_res = jnp.transpose(jnp.take(residual, row_idx, axis=1), (1, 0, 2))
    base_pts = node_pts
    half_s = SKELETON // 2
    node_pts = node_pts.reshape(N_CLUS, N_LEAF, FEATURES, SKELETON)
    node_res = node_res.reshape(N_CLUS, N_LEAF, RHS_COLS, SKELETON)
    solver = jax.vmap(jax.vmap(node_solve))
    stored = []
    for level_idx in range(LEVELS):
        solved = solver(node_pts, node_res)
        stored.append(solved)
        node_pts = jnp.concatenate([node_pts[:, 0::2, :, :half_s], node_pts[:, 1::2, :, :half_s]], axis=3)
        node_res = node_shift * jnp.concatenate([solved[:, 0::2, :, :half_s], solved[:, 1::2, :, :half_s]], axis=3)
    correction = solver(node_pts, node_res)
    for level_idx in reversed(range(LEVELS)):
        inject = jnp.stack([correction[..., :half_s], correction[..., half_s:]], axis=2)
        inject = inject.reshape(N_CLUS, -1, RHS_COLS, half_s)
        correction = stored[level_idx] + jnp.concatenate([inject, jnp.zeros_like(inject)], axis=3)
    return (base_pts, correction.reshape(DEVICES, RHS_COLS, SKELETON))

def prolong(dev_pts, dev_res, base_pts, correction, skel_row):
    tile_low = lax.optimization_barrier(kernel_tile(base_pts, dev_pts).astype(jnp.bfloat16))
    corr_low = lax.optimization_barrier(correction.astype(jnp.bfloat16))
    spread = jnp.dot(corr_low.astype(jnp.float32), tile_low.astype(jnp.float32), precision=lax.Precision.HIGHEST)
    result = dev_res / (1.0 + ridge_term) + spread
    return result.at[:, skel_row].add(correction)

def reference(points, weights, targets, near_lists, tile_counts, skeleton):
    near_sum = near_field(points, weights, near_lists, tile_counts)
    residual = targets.astype(jnp.float32) - ridge_term * weights.astype(jnp.float32) - near_sum
    base_pts, correction = tree_correction(points, residual, skeleton)

    def per_device(dev_idx):
        begin_col = (dev_idx * PTS_DEV).astype(jnp.int32)
        dev_pts = lax.dynamic_slice_in_dim(points, begin_col, PTS_DEV, 1)
        dev_res = lax.dynamic_slice_in_dim(residual, begin_col, PTS_DEV, 1)
        return prolong(dev_pts, dev_res, base_pts[dev_idx], correction[dev_idx], skeleton[dev_idx])
    blocks = lax.map(per_device, jnp.arange(DEVICES, dtype=jnp.int32))
    return jnp.transpose(blocks, (1, 0, 2)).reshape(RHS_COLS, POINTS)
```

```python
import functools

import jax
import jax.numpy as jnp
from jax import lax
from jax.experimental import pallas as pl
from jax.experimental.pallas import tpu as pltpu
from jax.sharding import PartitionSpec as P

ridge_term = 0.5
node_shift = 4.0
MESH = pl.DeviceIdType.MESH
F32 = jnp.float32
BF16 = jnp.bfloat16
SWEEP = 8
LOG2E = 1.4426950408889634
PIECE = 64
CHUNK = 128


def dot(a, b):
    return jnp.dot(a, b, preferred_element_type=F32)


def dot_full(a, b, dims=((1,), (0,))):
    return lax.dot_general(
        a, b, (dims, ((), ())), precision=lax.Precision.HIGHEST, preferred_element_type=F32
    )


def split(a):
    high = a.astype(BF16)
    return high, (a - high.astype(F32)).astype(BF16)


def dot_split(a, b_high, b_low):
    a_high, a_low = split(a)
    return dot(a_high, b_high) + dot(a_low, b_high) + dot(a_high, b_low)


def square_cols(pts):
    wide = pts.astype(F32)
    return dot_full(wide * wide, jnp.ones((pts.shape[0], 128), F32), ((0,), (0,)))


def square_rows(pts):
    wide = pts.astype(F32)
    return jnp.sum(wide * wide, axis=0, keepdims=True)


def kernel_tile(row_pts, row_sq, col_pts, col_sq, bias=0.0):
    scale = 2.0 / row_pts.shape[0] * LOG2E
    cross = lax.dot_general(
        row_pts, col_pts, (((0,), (0,)), ((), ())), preferred_element_type=F32
    )
    row_wide = jnp.concatenate([row_sq * -scale] * (col_pts.shape[1] // 128), axis=1)
    return jnp.exp2(cross * (2.0 * scale) + (row_wide + (col_sq * -scale + bias)))


def sweep_inverse(mats):
    count, size = mats.shape[0], mats.shape[1]
    row_id = lax.broadcasted_iota(jnp.int32, (count, size, 1), 1)
    col_id = lax.broadcasted_iota(jnp.int32, (count, 1, size), 2)

    def group(_, a):
        for i in range(SWEEP):
            row = a[:, i : i + 1, :]
            col = a[:, :, i : i + 1]
            inv = 1.0 / a[:, i : i + 1, i : i + 1]
            row = jnp.where(col_id == i, -inv, row * inv)
            col = jnp.where(row_id == i, -1.0, col)
            rest = jnp.where((row_id == i) | (col_id == i), 0.0, a)
            a = rest - col * row
        a = jnp.concatenate([a[:, SWEEP:, :], a[:, :SWEEP, :]], axis=1)
        return pltpu.roll(a, size - SWEEP, 2)

    return -lax.fori_loop(0, size // SWEEP, group, mats)


def fused_kernel(
    n_clus, n_leaf,
    points, weights, targets, bias, skeleton,
    out,
    window, win_p, win_sq, tiles, pick, prolong, gram, inv_high, inv_low, node_p, got_p,
    node_r, got_r, sent_r, solved_buf,
    ps, pr, as_, ar, bs, br, qs, qr, ts, tr,
):
    clus, leaf = lax.axis_index("clus"), lax.axis_index("leaf")
    levels = n_leaf.bit_length() - 1
    clusters = bias.shape[0] // 3
    pts_cl = points.shape[1] // clusters
    n_skel = skeleton.shape[1]
    half = n_skel // 2
    n_piece = weights.shape[0] // PIECE
    n_ch = weights.shape[0] // CHUNK
    even = lax.rem(clus, 2) == 0
    partner = jnp.where(even, clus + 1, clus - 1)
    onward = jnp.where(even, clus + 2, clus - 2)
    behind = jnp.where(even, clus - 2, clus + 2)
    has_onward = (onward >= 0) & (onward < n_clus)
    has_behind = (behind >= 0) & (behind < n_clus)
    siblings = []
    for level in range(levels):
        upper = lax.rem(leaf // (1 << level), 2) == 1
        siblings.append((upper, jnp.where(upper, leaf - (1 << level), leaf + (1 << level))))

    barrier = pltpu.get_barrier_semaphore()
    pl.semaphore_signal(barrier, inc=1, device_id=(partner, leaf), device_id_type=MESH)
    for _, sibling in siblings:
        pl.semaphore_signal(barrier, inc=1, device_id=(clus, sibling), device_id_type=MESH)

    @pl.when(has_onward)
    def _():
        pl.semaphore_signal(barrier, inc=1, device_id=(onward, leaf), device_id_type=MESH)

    @pl.when(has_behind)
    def _():
        pl.semaphore_signal(barrier, inc=1, device_id=(behind, leaf), device_id_type=MESH)

    pl.semaphore_wait(
        barrier, 1 + levels + has_onward.astype(jnp.int32) + has_behind.astype(jnp.int32)
    )

    def remote(src, dst, send, recv, where):
        return pltpu.make_async_remote_copy(
            src_ref=src, dst_ref=dst, send_sem=send, recv_sem=recv, device_id=where,
            device_id_type=MESH,
        )

    first_p = remote(points, win_p.at[1], ps.at[0], pr.at[0], (partner, leaf))
    next_p = remote(win_p.at[1], win_p.at[2], ps.at[1], pr.at[1], (onward, leaf))
    first_p.start()
    first_w, next_w = [], []
    for i in range(n_piece):
        rows = pl.ds(i * PIECE, PIECE)
        first_w.append(remote(
            weights.at[rows], window.at[0, rows], as_.at[i], ar.at[i], (partner, leaf)
        ))
        next_w.append(remote(
            window.at[0, rows], window.at[1, rows], bs.at[i], br.at[i], (onward, leaf)
        ))
        first_w[i].start()

    def pass_on(first, after):
        first.wait_recv()

        @pl.when(has_onward)
        def _():
            after.start()

    @pl.when(jnp.logical_not(has_behind))
    def _():
        win_p[2] = jnp.zeros(points.shape, BF16)
        window[1] = jnp.zeros(weights.shape, BF16)

    def take(after):
        @pl.when(has_behind)
        def _():
            after.wait_recv()

    skel = skeleton[...]
    pick[...] = (
        lax.broadcasted_iota(jnp.int32, (points.shape[1], n_skel), 0) == skel
    ).astype(BF16)
    base_p = dot(points[...], pick[...]).astype(BF16)
    node_p[0] = base_p
    for level, (upper, sibling) in enumerate(siblings):
        copy = remote(
            node_p.at[level, :, pl.ds(0, half)], got_p.at[level], qs.at[level], qr.at[level],
            (clus, sibling),
        )
        copy.start()
        copy.wait()
        mine, other = node_p[level, :, :half], got_p[level]
        node_p[level + 1, :, :half] = jnp.where(upper, other, mine)
        node_p[level + 1, :, half:] = jnp.where(upper, mine, other)

    pass_on(first_p, next_p)
    win_p[0] = points[...]
    for level in range(levels + 1):
        p = node_p[level]
        shift_mat = jnp.where(
            lax.broadcasted_iota(jnp.int32, (n_skel, n_skel), 0)
            == lax.broadcasted_iota(jnp.int32, (n_skel, n_skel), 1),
            node_shift, 0.0,
        )
        gram[level] = kernel_tile(p, square_cols(p), p, square_rows(p)) + shift_mat

    own_sq_cols = square_cols(base_p)
    own_sq = square_rows(points[...])
    for k in range(clusters):
        cols = slice(k * pts_cl, (k + 1) * pts_cl)
        prolong[:, cols] = kernel_tile(
            base_p, own_sq_cols, points[:, cols], own_sq[:, cols]
        ).astype(BF16)

    top_inv = sweep_inverse(gram[:, :half, :half])
    couple = [dot_full(top_inv[v], gram[v, :half, half:]) for v in range(levels + 1)]
    schur = jnp.stack([
        gram[v, half:, half:] - dot_full(gram[v, half:, :half], couple[v])
        for v in range(levels + 1)
    ])
    pass_on(first_w[0], next_w[0])
    pass_on(first_w[1], next_w[1])
    low_inv = sweep_inverse(schur)
    pass_on(first_w[2], next_w[2])
    pass_on(first_w[3], next_w[3])
    for v in range(levels + 1):
        cross = dot_full(couple[v], low_inv[v])
        corner = top_inv[v] + dot_full(cross, couple[v], ((1,), (1,)))
        whole = jnp.concatenate([
            jnp.concatenate([corner, -cross], axis=1),
            jnp.concatenate([-cross.T, low_inv[v]], axis=1),
        ], axis=0)
        inv_high[v], inv_low[v] = split(whole)

    take(next_p)
    for place in range(3):
        win_sq[...] = square_cols(win_p[place])

        def build(r, _):
            rows = pl.ds(pl.multiple_of(r * 128, 128), 128)
            q = pl.ds(place * clusters + r * 128 // pts_cl, 1)
            for k in range(clusters):
                cols = slice(k * pts_cl, (k + 1) * pts_cl)
                tiles[place, rows, cols] = kernel_tile(
                    win_p[place, :, rows], win_sq[rows, :],
                    points[:, cols], own_sq[:, cols], bias[q, cols],
                ).astype(BF16)
            return 0

        lax.fori_loop(0, points.shape[1] // 128, build, 0)

    per = CHUNK // PIECE
    passed = 4

    def exchange(c, level):
        at = c * levels + level
        return remote(
            sent_r.at[at], got_r.at[at], ts.at[at], tr.at[at], (clus, siblings[level][1])
        )

    def climb(c, level, node_res):
        solved = dot_split(node_res, inv_high[level], inv_low[level])
        solved_buf[c * levels + level] = solved
        sent_r[c * levels + level] = node_shift * solved[:, :half]
        exchange(c, level).start()

    def joined(c, level):
        exchange(c, level).wait()
        mine, other = sent_r[c * levels + level], got_r[c * levels + level]
        upper = siblings[level][0]
        return jnp.concatenate(
            [jnp.where(upper, other, mine), jnp.where(upper, mine, other)], axis=1
        )

    def near_stage(c):
        span = slice(c * CHUNK, (c + 1) * CHUNK)
        for i in range(max(passed, c * per), (c + 1) * per):
            pass_on(first_w[i], next_w[i])
        @pl.loop(0, clusters)
        def _(k):
            cols = pl.ds(pl.multiple_of(k * pts_cl, pts_cl), pts_cl)
            near = dot(weights[span, :], tiles[0, :, cols]) + dot(
                window[0, span, :], tiles[1, :, cols]
            )
            out[span, cols] = (
                targets[span, cols].astype(F32) - ridge_term * weights[span, cols].astype(F32)
                - near
            )
        for i in range(c * per, (c + 1) * per):
            take(next_w[i])
        node_r[...] = jnp.zeros_like(node_r)

        @pl.loop(0, clusters)
        def _(k):
            cols = pl.ds(pl.multiple_of(k * pts_cl, pts_cl), pts_cl)
            residual = out[span, cols] - dot(window[1, span, :], tiles[2, :, cols])
            out[span, cols] = residual
            high, low = split(residual)
            node_r[...] += dot(high, pick[cols, :]) + dot(low, pick[cols, :])
        climb(c, 0, node_r[...])

    def last_stage(c):
        span = slice(c * CHUNK, (c + 1) * CHUNK)
        correction = dot_split(joined(c, levels - 1), inv_high[levels], inv_low[levels])
        for level in reversed(range(levels)):
            upper = siblings[level][0]
            inject = jnp.where(upper, correction[:, half:], correction[:, :half])
            correction = solved_buf[c * levels + level] + jnp.concatenate(
                [inject, jnp.zeros_like(inject)], axis=1
            )
        high, low = split(correction)

        @pl.loop(0, clusters)
        def _(k):
            cols = pl.ds(pl.multiple_of(k * pts_cl, pts_cl), pts_cl)
            placed = lax.dot_general(
                jnp.concatenate([high, low], axis=0), pick[cols, :], (((1,), (1,)), ((), ())),
                preferred_element_type=F32,
            )
            out[span, cols] = (
                out[span, cols] * (1.0 / (1.0 + ridge_term)) + dot(high, prolong[:, cols])
                + (placed[:CHUNK] + placed[CHUNK:])
            )

    for step in range(n_ch + levels):
        for stage in reversed(range(levels + 1)):
            c = step - stage
            if not 0 <= c < n_ch:
                continue
            if stage == 0:
                near_stage(c)
            elif stage < levels:
                climb(c, stage, joined(c, stage - 1))
            else:
                last_stage(c)

    first_p.wait_send()
    for i in range(n_piece):
        first_w[i].wait_send()

    @pl.when(has_onward)
    def _():
        next_p.wait_send()
        for i in range(n_piece):
            next_w[i].wait_send()


def near_bias(n_clus, n_leaf, pts_cl, near_lists, tile_counts):
    clus, leaf = lax.axis_index("clus"), lax.axis_index("leaf")
    clusters, slots = near_lists.shape
    even = lax.rem(clus, 2) == 0
    partner = jnp.where(even, clus + 1, clus - 1)
    other = jnp.where(even, clus - 1, clus + 1)
    place = jnp.stack([clus, partner, other])
    valid = (place >= 0) & (place < n_clus)
    first = jnp.where(valid, (place * n_leaf + leaf) * clusters, -clusters)
    ident = (first[:, None] + jnp.arange(clusters)[None, :]).reshape(-1)
    used = jnp.arange(slots)[None, :] < tile_counts[:, None]
    hit = (near_lists[:, :, None] == ident[None, None, :]) & used[:, :, None]
    bias = jnp.where(jnp.any(hit, axis=1), 0.0, -1e30).astype(F32)
    return jnp.repeat(bias.T, pts_cl, axis=1)


def on_device(n_clus, n_leaf, points, weights, targets, near_lists, tile_counts, skeleton):
    rhs, pts = weights.shape
    features = points.shape[0]
    clusters = near_lists.shape[0]
    n_skel = skeleton.shape[1]
    half = n_skel // 2
    levels = n_leaf.bit_length() - 1
    n_piece, n_ch = rhs // PIECE, rhs // CHUNK
    vmem = pl.BlockSpec(memory_space=pltpu.VMEM)
    dma = pltpu.SemaphoreType.DMA
    bias = near_bias(n_clus, n_leaf, pts // clusters, near_lists, tile_counts)
    return pl.pallas_call(
        functools.partial(fused_kernel, n_clus, n_leaf),
        out_shape=jax.ShapeDtypeStruct((rhs, pts), F32),
        in_specs=[vmem] * 5,
        out_specs=vmem,
        scratch_shapes=[
            pltpu.VMEM((2, rhs, pts), BF16),
            pltpu.VMEM((3, features, pts), BF16),
            pltpu.VMEM((pts, 128), F32),
            pltpu.VMEM((3, pts, pts), BF16),
            pltpu.VMEM((pts, n_skel), BF16),
            pltpu.VMEM((n_skel, pts), BF16),
            pltpu.VMEM((levels + 1, n_skel, n_skel), F32),
            pltpu.VMEM((levels + 1, n_skel, n_skel), BF16),
            pltpu.VMEM((levels + 1, n_skel, n_skel), BF16),
            pltpu.VMEM((levels + 1, features, n_skel), BF16),
            pltpu.VMEM((levels, features, half), BF16),
            pltpu.VMEM((CHUNK, n_skel), F32),
            pltpu.VMEM((n_ch * levels, CHUNK, half), F32),
            pltpu.VMEM((n_ch * levels, CHUNK, half), F32),
            pltpu.VMEM((n_ch * levels, CHUNK, n_skel), F32),
            dma((2,)), dma((2,)),
            dma((n_piece,)), dma((n_piece,)), dma((n_piece,)), dma((n_piece,)),
            dma((levels,)), dma((levels,)),
            dma((n_ch * levels,)), dma((n_ch * levels,)),
        ],
        compiler_params=pltpu.CompilerParams(
            collective_id=0, has_side_effects=True, vmem_limit_bytes=60 * 1024 * 1024
        ),
    )(points, weights, targets, bias, skeleton)


def solution(mesh):
    placed = (
        P(None, ("clus", "leaf")),
        P(None, ("clus", "leaf")),
        P(None, ("clus", "leaf")),
        P(("clus", "leaf"), None),
        P(("clus", "leaf")),
        P(("clus", "leaf"), None),
    )
    return jax.shard_map(
        functools.partial(on_device, mesh.shape["clus"], mesh.shape["leaf"]),
        mesh=mesh, in_specs=placed, out_specs=P(None, ("clus", "leaf")), check_vma=False,
    )
```

```python
import functools

import jax
import jax.numpy as jnp
from jax import lax
from jax.experimental import pallas as pl
from jax.experimental.pallas import tpu as pltpu
from jax.sharding import PartitionSpec as P

ridge_term = 0.5
node_shift = 4.0
MESH = pl.DeviceIdType.MESH
F32 = jnp.float32
BF16 = jnp.bfloat16
SWEEP = 8
LOG2E = 1.4426950408889634
PIECE = 64
CHUNK = 128


def dot(a, b):
    return jnp.dot(a, b, preferred_element_type=F32)


def dot_full(a, b, dims=((1,), (0,))):
    return lax.dot_general(
        a, b, (dims, ((), ())), precision=lax.Precision.HIGHEST, preferred_element_type=F32
    )


def split(a):
    high = a.astype(BF16)
    return high, (a - high.astype(F32)).astype(BF16)


def dot_split(a, b_high, b_low):
    a_high, a_low = split(a)
    return dot(a_high, b_high) + dot(a_low, b_high) + dot(a_high, b_low)


def square_cols(pts):
    wide = pts.astype(F32)
    return dot_full(wide * wide, jnp.ones((pts.shape[0], 128), F32), ((0,), (0,)))


def square_rows(pts):
    wide = pts.astype(F32)
    return jnp.sum(wide * wide, axis=0, keepdims=True)


def kernel_tile(row_pts, row_sq, col_pts, col_sq, bias=0.0):
    scale = 2.0 / row_pts.shape[0] * LOG2E
    cross = lax.dot_general(
        row_pts, col_pts, (((0,), (0,)), ((), ())), preferred_element_type=F32
    )
    row_wide = jnp.concatenate([row_sq * -scale] * (col_pts.shape[1] // 128), axis=1)
    return jnp.exp2(cross * (2.0 * scale) + (row_wide + (col_sq * -scale + bias)))


def sweep_inverse(mats, beside):
    count, size = mats.shape[0], mats.shape[1]
    row_id = lax.broadcasted_iota(jnp.int32, (count, SWEEP, 1), 1)
    col_id = lax.broadcasted_iota(jnp.int32, (count, 1, size), 2)

    def group(step, a):
        beside(step)
        panel = a[:, :SWEEP, :]
        for i in range(SWEEP):
            row = panel[:, i : i + 1, :]
            col = panel[:, :, i : i + 1]
            inv = 1.0 / panel[:, i : i + 1, i : i + 1]
            row = jnp.where(col_id == i, -inv, row * inv)
            col = jnp.where(row_id == i, -1.0, col)
            panel = jnp.where((row_id == i) | (col_id == i), 0.0, panel) - col * row
        below = a[:, SWEEP:, :]
        rest = jnp.where(col_id < SWEEP, 0.0, below)
        for i in range(SWEEP):
            rest = rest - below[:, :, i : i + 1] * panel[:, i : i + 1, :]
        return pltpu.roll(jnp.concatenate([rest, panel], axis=1), size - SWEEP, 2)

    return -lax.fori_loop(0, size // SWEEP, group, mats)


def fused_kernel(
    n_clus, n_leaf,
    points, weights, targets, near_lists, tile_counts, skeleton,
    out,
    bias, window, win_p, win_sq, tiles, pick, prolong, gram, inv_high, inv_low, node_p, got_p,
    node_r, got_r, sent_r, solved_buf,
    ps, pr, as_, ar, bs, br, qs, qr, ts, tr,
):
    clus, leaf = lax.axis_index("clus"), lax.axis_index("leaf")
    levels = n_leaf.bit_length() - 1
    clusters, slots = near_lists.shape
    pts_cl = points.shape[1] // clusters
    n_skel = skeleton.shape[1]
    half = n_skel // 2
    n_piece = weights.shape[0] // PIECE
    n_ch = weights.shape[0] // CHUNK
    even = lax.rem(clus, 2) == 0
    partner = jnp.where(even, clus + 1, clus - 1)
    onward = jnp.where(even, clus + 2, clus - 2)
    behind = jnp.where(even, clus - 2, clus + 2)
    has_onward = (onward >= 0) & (onward < n_clus)
    has_behind = (behind >= 0) & (behind < n_clus)
    siblings = []
    for level in range(levels):
        upper = lax.rem(leaf // (1 << level), 2) == 1
        siblings.append((upper, jnp.where(upper, leaf - (1 << level), leaf + (1 << level))))

    barrier = pltpu.get_barrier_semaphore()
    pl.semaphore_signal(barrier, inc=1, device_id=(partner, leaf), device_id_type=MESH)
    for _, sibling in siblings:
        pl.semaphore_signal(barrier, inc=1, device_id=(clus, sibling), device_id_type=MESH)

    @pl.when(has_onward)
    def _():
        pl.semaphore_signal(barrier, inc=1, device_id=(onward, leaf), device_id_type=MESH)

    @pl.when(has_behind)
    def _():
        pl.semaphore_signal(barrier, inc=1, device_id=(behind, leaf), device_id_type=MESH)

    pl.semaphore_wait(
        barrier, 1 + levels + has_onward.astype(jnp.int32) + has_behind.astype(jnp.int32)
    )

    def remote(src, dst, send, recv, where):
        return pltpu.make_async_remote_copy(
            src_ref=src, dst_ref=dst, send_sem=send, recv_sem=recv, device_id=where,
            device_id_type=MESH,
        )

    first_p = remote(points, win_p.at[1], ps.at[0], pr.at[0], (partner, leaf))
    next_p = remote(win_p.at[1], win_p.at[2], ps.at[1], pr.at[1], (onward, leaf))
    first_p.start()
    first_w, next_w = [], []
    for i in range(n_piece):
        rows = pl.ds(i * PIECE, PIECE)
        first_w.append(remote(
            weights.at[rows], window.at[0, rows], as_.at[i], ar.at[i], (partner, leaf)
        ))
        next_w.append(remote(
            window.at[0, rows], window.at[1, rows], bs.at[i], br.at[i], (onward, leaf)
        ))
        first_w[i].start()

    def pass_on(first, after):
        first.wait_recv()

        @pl.when(has_onward)
        def _():
            after.start()

    @pl.when(jnp.logical_not(has_behind))
    def _():
        win_p[2] = jnp.zeros(points.shape, BF16)
        window[1] = jnp.zeros(weights.shape, BF16)

    def take(after):
        @pl.when(has_behind)
        def _():
            after.wait_recv()

    spot = lax.broadcasted_iota(jnp.int32, (3 * clusters, 1), 0)
    place_clus = jnp.where(
        spot < clusters, clus,
        jnp.where(spot < 2 * clusters, partner, jnp.where(even, clus - 1, clus + 1)),
    )
    spot_id = (place_clus * n_leaf + leaf) * clusters + lax.rem(spot, clusters)
    spot_id = jnp.where((place_clus >= 0) & (place_clus < n_clus), spot_id, -1)
    for k in range(clusters):
        miss = jnp.full((3 * clusters, 1), -1e30, F32)
        for s in range(slots):
            hit = (spot_id == near_lists[k : k + 1, s : s + 1]) & (s < tile_counts[:, k : k + 1])
            miss = jnp.where(hit, 0.0, miss)
        bias[:, k * pts_cl : (k + 1) * pts_cl] = jnp.broadcast_to(miss, (3 * clusters, pts_cl))

    skel = skeleton[...]
    pick[...] = (
        lax.broadcasted_iota(jnp.int32, (points.shape[1], n_skel), 0) == skel
    ).astype(BF16)
    base_p = dot(points[...], pick[...]).astype(BF16)
    node_p[0] = base_p
    for level, (upper, sibling) in enumerate(siblings):
        copy = remote(
            node_p.at[level, :, pl.ds(0, half)], got_p.at[level], qs.at[level], qr.at[level],
            (clus, sibling),
        )
        copy.start()
        copy.wait()
        mine, other = node_p[level, :, :half], got_p[level]
        node_p[level + 1, :, :half] = jnp.where(upper, other, mine)
        node_p[level + 1, :, half:] = jnp.where(upper, mine, other)

    pass_on(first_p, next_p)
    win_p[0] = points[...]
    for level in range(levels + 1):
        p = node_p[level]
        shift_mat = jnp.where(
            lax.broadcasted_iota(jnp.int32, (n_skel, n_skel), 0)
            == lax.broadcasted_iota(jnp.int32, (n_skel, n_skel), 1),
            node_shift, 0.0,
        )
        gram[level] = kernel_tile(p, square_cols(p), p, square_rows(p)) + shift_mat

    own_sq_cols = square_cols(base_p)
    own_sq = square_rows(points[...])
    for k in range(clusters):
        cols = slice(k * pts_cl, (k + 1) * pts_cl)
        prolong[:, cols] = kernel_tile(
            base_p, own_sq_cols, points[:, cols], own_sq[:, cols]
        ).astype(BF16)

    def build(place, r):
        rows = pl.ds(pl.multiple_of(r * 128, 128), 128)
        q = pl.ds(place * clusters + r * 128 // pts_cl, 1)
        for k in range(clusters):
            cols = slice(k * pts_cl, (k + 1) * pts_cl)
            tiles[place, rows, cols] = kernel_tile(
                win_p[place, :, rows], win_sq[place, rows, :],
                points[:, cols], own_sq[:, cols], bias[q, cols],
            ).astype(BF16)

    n_block = points.shape[1] // 128
    n_step = half // SWEEP
    per_step = -(-n_block // n_step)

    def beside_top(step):
        for t in range(per_step):
            build(0, step * per_step + t)
            build(1, step * per_step + t)

    own_rows = weights.shape[0] * clusters // n_step

    def beside_low(step):
        for t in range(per_step):
            build(2, step * per_step + t)
        span = pl.ds(pl.multiple_of(step // clusters * own_rows, own_rows), own_rows)
        cols = pl.ds(pl.multiple_of(lax.rem(step, clusters) * pts_cl, pts_cl), pts_cl)
        out[span, cols] = (
            targets[span, cols].astype(F32) - ridge_term * weights[span, cols].astype(F32)
            - dot(weights[span, :], tiles[0, :, cols])
        )

    win_sq[0] = square_cols(win_p[0])
    win_sq[1] = square_cols(win_p[1])
    top_inv = sweep_inverse(gram[:, :half, :half], beside_top)
    pass_on(first_w[0], next_w[0])
    take(next_p)
    win_sq[2] = square_cols(win_p[2])
    couple = [dot_full(top_inv[v], gram[v, :half, half:]) for v in range(levels + 1)]
    schur = jnp.stack([
        gram[v, half:, half:] - dot_full(gram[v, half:, :half], couple[v])
        for v in range(levels + 1)
    ])
    pass_on(first_w[1], next_w[1])
    pass_on(first_w[2], next_w[2])
    low_inv = sweep_inverse(schur, beside_low)
    pass_on(first_w[3], next_w[3])
    pass_on(first_w[4], next_w[4])
    for v in range(levels + 1):
        cross = dot_full(couple[v], low_inv[v])
        corner = top_inv[v] + dot_full(cross, couple[v], ((1,), (1,)))
        whole = jnp.concatenate([
            jnp.concatenate([corner, -cross], axis=1),
            jnp.concatenate([-cross.T, low_inv[v]], axis=1),
        ], axis=0)
        inv_high[v], inv_low[v] = split(whole)

    per = CHUNK // PIECE
    passed = 5
    for c in range(n_ch):
        span = slice(c * CHUNK, (c + 1) * CHUNK)
        while passed < n_piece and passed < max((c + 1) * per, 6 + c):
            pass_on(first_w[passed], next_w[passed])
            passed += 1

        @pl.loop(0, clusters)
        def _(k):
            cols = pl.ds(pl.multiple_of(k * pts_cl, pts_cl), pts_cl)
            out[span, cols] -= dot(window[0, span, :], tiles[1, :, cols])

    def exchange(c, level):
        at = c * levels + level
        return remote(
            sent_r.at[at], got_r.at[at], ts.at[at], tr.at[at], (clus, siblings[level][1])
        )

    def climb(c, level, node_res):
        solved = dot_split(node_res, inv_high[level], inv_low[level])
        solved_buf[c * levels + level] = solved
        sent_r[c * levels + level] = node_shift * solved[:, :half]
        exchange(c, level).start()

    def joined(c, level):
        exchange(c, level).wait()
        mine, other = sent_r[c * levels + level], got_r[c * levels + level]
        upper = siblings[level][0]
        return jnp.concatenate(
            [jnp.where(upper, other, mine), jnp.where(upper, mine, other)], axis=1
        )

    def near_stage(c):
        span = slice(c * CHUNK, (c + 1) * CHUNK)
        for i in range(c * per, (c + 1) * per):
            take(next_w[i])
        node_r[...] = jnp.zeros_like(node_r)

        @pl.loop(0, clusters)
        def _(k):
            cols = pl.ds(pl.multiple_of(k * pts_cl, pts_cl), pts_cl)
            residual = out[span, cols] - dot(window[1, span, :], tiles[2, :, cols])
            out[span, cols] = residual
            high, low = split(residual)
            node_r[...] += dot(high, pick[cols, :]) + dot(low, pick[cols, :])
        climb(c, 0, node_r[...])

    def last_stage(c):
        span = slice(c * CHUNK, (c + 1) * CHUNK)
        correction = dot_split(joined(c, levels - 1), inv_high[levels], inv_low[levels])
        for level in reversed(range(levels)):
            upper = siblings[level][0]
            inject = jnp.where(upper, correction[:, half:], correction[:, :half])
            correction = solved_buf[c * levels + level] + jnp.concatenate(
                [inject, jnp.zeros_like(inject)], axis=1
            )
        high, low = split(correction)

        @pl.loop(0, clusters)
        def _(k):
            cols = pl.ds(pl.multiple_of(k * pts_cl, pts_cl), pts_cl)
            placed = lax.dot_general(
                jnp.concatenate([high, low], axis=0), pick[cols, :], (((1,), (1,)), ((), ())),
                preferred_element_type=F32,
            )
            out[span, cols] = (
                out[span, cols] * (1.0 / (1.0 + ridge_term)) + dot(high, prolong[:, cols])
                + (placed[:CHUNK] + placed[CHUNK:])
            )

    for step in range(n_ch + levels):
        for stage in reversed(range(levels + 1)):
            c = step - stage
            if not 0 <= c < n_ch:
                continue
            if stage == 0:
                near_stage(c)
            elif stage < levels:
                climb(c, stage, joined(c, stage - 1))
            else:
                last_stage(c)

    first_p.wait_send()
    for i in range(n_piece):
        first_w[i].wait_send()

    @pl.when(has_onward)
    def _():
        next_p.wait_send()
        for i in range(n_piece):
            next_w[i].wait_send()


def on_device(n_clus, n_leaf, points, weights, targets, near_lists, tile_counts, skeleton):
    rhs, pts = weights.shape
    features = points.shape[0]
    clusters = near_lists.shape[0]
    n_skel = skeleton.shape[1]
    half = n_skel // 2
    levels = n_leaf.bit_length() - 1
    n_piece, n_ch = rhs // PIECE, rhs // CHUNK
    vmem = pl.BlockSpec(memory_space=pltpu.VMEM)
    dma = pltpu.SemaphoreType.DMA
    return pl.pallas_call(
        functools.partial(fused_kernel, n_clus, n_leaf),
        out_shape=jax.ShapeDtypeStruct((rhs, pts), F32),
        in_specs=[vmem] * 6,
        out_specs=vmem,
        scratch_shapes=[
            pltpu.VMEM((3 * clusters, pts), F32),
            pltpu.VMEM((2, rhs, pts), BF16),
            pltpu.VMEM((3, features, pts), BF16),
            pltpu.VMEM((3, pts, 128), F32),
            pltpu.VMEM((3, pts, pts), BF16),
            pltpu.VMEM((pts, n_skel), BF16),
            pltpu.VMEM((n_skel, pts), BF16),
            pltpu.VMEM((levels + 1, n_skel, n_skel), F32),
            pltpu.VMEM((levels + 1, n_skel, n_skel), BF16),
            pltpu.VMEM((levels + 1, n_skel, n_skel), BF16),
            pltpu.VMEM((levels + 1, features, n_skel), BF16),
            pltpu.VMEM((levels, features, half), BF16),
            pltpu.VMEM((CHUNK, n_skel), F32),
            pltpu.VMEM((n_ch * levels, CHUNK, half), F32),
            pltpu.VMEM((n_ch * levels, CHUNK, half), F32),
            pltpu.VMEM((n_ch * levels, CHUNK, n_skel), F32),
            dma((2,)), dma((2,)),
            dma((n_piece,)), dma((n_piece,)), dma((n_piece,)), dma((n_piece,)),
            dma((levels,)), dma((levels,)),
            dma((n_ch * levels,)), dma((n_ch * levels,)),
        ],
        compiler_params=pltpu.CompilerParams(
            collective_id=0, has_side_effects=True, vmem_limit_bytes=60 * 1024 * 1024
        ),
    )(points, weights, targets, near_lists, tile_counts.reshape(1, -1), skeleton)


def solution(mesh):
    placed = (
        P(None, ("clus", "leaf")),
        P(None, ("clus", "leaf")),
        P(None, ("clus", "leaf")),
        P(("clus", "leaf"), None),
        P(("clus", "leaf")),
        P(("clus", "leaf"), None),
    )
    return jax.shard_map(
        functools.partial(on_device, mesh.shape["clus"], mesh.shape["leaf"]),
        mesh=mesh, in_specs=placed, out_specs=P(None, ("clus", "leaf")), check_vma=False,
    )
```

```python
import functools

import jax
import jax.numpy as jnp
from jax import lax
from jax.experimental import pallas as pl
from jax.experimental.pallas import tpu as pltpu
from jax.sharding import PartitionSpec as P

ridge_term = 0.5
node_shift = 4.0
MESH = pl.DeviceIdType.MESH
F32 = jnp.float32
BF16 = jnp.bfloat16
SWEEP = 8
LOG2E = 1.4426950408889634
PIECE = 64
CHUNK = 256


def dot(a, b):
    return jnp.dot(a, b, preferred_element_type=F32)


def dot_full(a, b, dims=((1,), (0,))):
    return lax.dot_general(
        a, b, (dims, ((), ())), precision=lax.Precision.HIGHEST, preferred_element_type=F32
    )


def split(a):
    high = a.astype(BF16)
    return high, (a - high.astype(F32)).astype(BF16)


def dot_split(a, b_high, b_low):
    a_high, a_low = split(a)
    return dot(a_high, b_high) + dot(a_low, b_high) + dot(a_high, b_low)


def square_cols(pts):
    wide = pts.astype(F32)
    return dot_full(wide * wide, jnp.ones((pts.shape[0], 128), F32), ((0,), (0,)))


def square_rows(pts):
    wide = pts.astype(F32)
    return jnp.sum(wide * wide, axis=0, keepdims=True)


def kernel_tile(row_pts, row_sq, col_pts, col_sq, bias=0.0):
    scale = 2.0 / row_pts.shape[0] * LOG2E
    cross = lax.dot_general(
        row_pts, col_pts, (((0,), (0,)), ((), ())), preferred_element_type=F32
    )
    row_wide = jnp.concatenate([row_sq * -scale] * (col_pts.shape[1] // 128), axis=1)
    return jnp.exp2(cross * (2.0 * scale) + (row_wide + (col_sq * -scale + bias)))


def sweep_inverse(mats, beside):
    count, size = mats.shape[0], mats.shape[1]
    row_id = lax.broadcasted_iota(jnp.int32, (count, SWEEP, 1), 1)
    col_id = lax.broadcasted_iota(jnp.int32, (count, 1, size), 2)

    def group(step, a):
        beside(step)
        panel = a[:, :SWEEP, :]
        for i in range(0, SWEEP, 2):
            row0, row1 = panel[:, i : i + 1, :], panel[:, i + 1 : i + 2, :]
            col0, col1 = panel[:, :, i : i + 1], panel[:, :, i + 1 : i + 2]
            p00, p01, p11 = row0[:, :, i : i + 1], row0[:, :, i + 1 : i + 2], row1[:, :, i + 1 : i + 2]
            inv = 1.0 / (p00 * p11 - p01 * p01)
            i00, i01, i11 = p11 * inv, -p01 * inv, p00 * inv
            new0 = i00 * row0 + i01 * row1
            new1 = i01 * row0 + i11 * row1
            new0 = jnp.where(col_id == i, -i00, jnp.where(col_id == i + 1, -i01, new0))
            new1 = jnp.where(col_id == i, -i01, jnp.where(col_id == i + 1, -i11, new1))
            row_in = (row_id == i) | (row_id == i + 1)
            col_in = (col_id == i) | (col_id == i + 1)
            col0 = jnp.where(row_in, jnp.where(row_id == i, -1.0, 0.0), col0)
            col1 = jnp.where(row_in, jnp.where(row_id == i, 0.0, -1.0), col1)
            panel = jnp.where(row_in | col_in, 0.0, panel) - col0 * new0 - col1 * new1
        below = a[:, SWEEP:, :]
        rest = jnp.where(col_id < SWEEP, 0.0, below)
        for i in range(SWEEP):
            rest = rest - below[:, :, i : i + 1] * panel[:, i : i + 1, :]
        return pltpu.roll(jnp.concatenate([rest, panel], axis=1), size - SWEEP, 2)

    return -lax.fori_loop(0, size // SWEEP, group, mats)


def fused_kernel(
    n_clus, n_leaf,
    points, weights, targets, near_lists, tile_counts, skeleton,
    out,
    bias, window, win_p, win_sq, tiles, pick, prolong, gram, inv_high, inv_low, node_p, got_p,
    node_r, got_r, sent_r, solved_buf,
    ps, pr, as_, ar, bs, br, qs, qr, ts, tr,
):
    clus, leaf = lax.axis_index("clus"), lax.axis_index("leaf")
    levels = n_leaf.bit_length() - 1
    clusters, slots = near_lists.shape
    pts_cl = points.shape[1] // clusters
    n_skel = skeleton.shape[1]
    half = n_skel // 2
    n_piece = weights.shape[0] // PIECE
    n_ch = weights.shape[0] // CHUNK
    even = lax.rem(clus, 2) == 0
    partner = jnp.where(even, clus + 1, clus - 1)
    onward = jnp.where(even, clus + 2, clus - 2)
    behind = jnp.where(even, clus - 2, clus + 2)
    has_onward = (onward >= 0) & (onward < n_clus)
    has_behind = (behind >= 0) & (behind < n_clus)
    siblings = []
    for level in range(levels):
        upper = lax.rem(leaf // (1 << level), 2) == 1
        siblings.append((upper, jnp.where(upper, leaf - (1 << level), leaf + (1 << level))))

    barrier = pltpu.get_barrier_semaphore()
    pl.semaphore_signal(barrier, inc=1, device_id=(partner, leaf), device_id_type=MESH)
    for _, sibling in siblings:
        pl.semaphore_signal(barrier, inc=1, device_id=(clus, sibling), device_id_type=MESH)

    @pl.when(has_onward)
    def _():
        pl.semaphore_signal(barrier, inc=1, device_id=(onward, leaf), device_id_type=MESH)

    @pl.when(has_behind)
    def _():
        pl.semaphore_signal(barrier, inc=1, device_id=(behind, leaf), device_id_type=MESH)

    pl.semaphore_wait(
        barrier, 1 + levels + has_onward.astype(jnp.int32) + has_behind.astype(jnp.int32)
    )

    def remote(src, dst, send, recv, where):
        return pltpu.make_async_remote_copy(
            src_ref=src, dst_ref=dst, send_sem=send, recv_sem=recv, device_id=where,
            device_id_type=MESH,
        )

    first_p = remote(points, win_p.at[1], ps.at[0], pr.at[0], (partner, leaf))
    next_p = remote(win_p.at[1], win_p.at[2], ps.at[1], pr.at[1], (onward, leaf))
    first_p.start()
    first_w, next_w = [], []
    for i in range(n_piece):
        rows = pl.ds(i * PIECE, PIECE)
        first_w.append(remote(
            weights.at[rows], window.at[0, rows], as_.at[i], ar.at[i], (partner, leaf)
        ))
        next_w.append(remote(
            window.at[0, rows], window.at[1, rows], bs.at[i], br.at[i], (onward, leaf)
        ))
        first_w[i].start()

    def pass_on(first, after):
        first.wait_recv()

        @pl.when(has_onward)
        def _():
            after.start()

    @pl.when(jnp.logical_not(has_behind))
    def _():
        win_p[2] = jnp.zeros(points.shape, BF16)
        window[1] = jnp.zeros(weights.shape, BF16)

    def take(after):
        @pl.when(has_behind)
        def _():
            after.wait_recv()

    spot = lax.broadcasted_iota(jnp.int32, (3 * clusters, 1), 0)
    place_clus = jnp.where(
        spot < clusters, clus,
        jnp.where(spot < 2 * clusters, partner, jnp.where(even, clus - 1, clus + 1)),
    )
    spot_id = (place_clus * n_leaf + leaf) * clusters + lax.rem(spot, clusters)
    spot_id = jnp.where((place_clus >= 0) & (place_clus < n_clus), spot_id, -1)
    for k in range(clusters):
        miss = jnp.full((3 * clusters, 1), -1e30, F32)
        for s in range(slots):
            hit = (spot_id == near_lists[k : k + 1, s : s + 1]) & (s < tile_counts[:, k : k + 1])
            miss = jnp.where(hit, 0.0, miss)
        bias[:, k * pts_cl : (k + 1) * pts_cl] = jnp.broadcast_to(miss, (3 * clusters, pts_cl))

    skel = skeleton[...]
    pick[...] = (
        lax.broadcasted_iota(jnp.int32, (points.shape[1], n_skel), 0) == skel
    ).astype(BF16)
    base_p = dot(points[...], pick[...]).astype(BF16)
    node_p[0] = base_p
    own_sq_cols = square_cols(base_p)
    own_sq = square_rows(points[...])

    def build_prolong(k):
        cols = slice(k * pts_cl, (k + 1) * pts_cl)
        prolong[:, cols] = kernel_tile(
            base_p, own_sq_cols, points[:, cols], own_sq[:, cols]
        ).astype(BF16)

    for level, (upper, sibling) in enumerate(siblings):
        copy = remote(
            node_p.at[level, :, pl.ds(0, half)], got_p.at[level], qs.at[level], qr.at[level],
            (clus, sibling),
        )
        copy.start()
        if level < clusters - 1:
            build_prolong(level)
        copy.wait()
        mine, other = node_p[level, :, :half], got_p[level]
        node_p[level + 1, :, :half] = jnp.where(upper, other, mine)
        node_p[level + 1, :, half:] = jnp.where(upper, mine, other)

    for k in range(min(levels, clusters - 1), clusters):
        build_prolong(k)
    pass_on(first_p, next_p)
    win_p[0] = points[...]
    for level in range(levels + 1):
        p = node_p[level]
        shift_mat = jnp.where(
            lax.broadcasted_iota(jnp.int32, (n_skel, n_skel), 0)
            == lax.broadcasted_iota(jnp.int32, (n_skel, n_skel), 1),
            node_shift, 0.0,
        )
        gram[level] = kernel_tile(p, square_cols(p), p, square_rows(p)) + shift_mat

    def build(place, r):
        rows = pl.ds(pl.multiple_of(r * 128, 128), 128)
        q = pl.ds(place * clusters + r * 128 // pts_cl, 1)
        for k in range(clusters):
            cols = slice(k * pts_cl, (k + 1) * pts_cl)
            tiles[place, rows, cols] = kernel_tile(
                win_p[place, :, rows], win_sq[place, rows, :],
                points[:, cols], own_sq[:, cols], bias[q, cols],
            ).astype(BF16)

    n_block = points.shape[1] // 128
    n_step = half // SWEEP
    per_step = -(-n_block // n_step)

    def beside_top(step):
        for t in range(per_step):
            build(0, step * per_step + t)
            build(1, step * per_step + t)

    own_rows = weights.shape[0] * clusters // n_step

    def beside_low(step):
        for t in range(per_step):
            build(2, step * per_step + t)
        span = pl.ds(pl.multiple_of(step // clusters * own_rows, own_rows), own_rows)
        cols = pl.ds(pl.multiple_of(lax.rem(step, clusters) * pts_cl, pts_cl), pts_cl)
        out[span, cols] = (
            targets[span, cols].astype(F32) - ridge_term * weights[span, cols].astype(F32)
            - dot(weights[span, :], tiles[0, :, cols])
        )

    win_sq[0] = square_cols(win_p[0])
    win_sq[1] = square_cols(win_p[1])
    top_inv = sweep_inverse(gram[:, :half, :half], beside_top)
    pass_on(first_w[0], next_w[0])
    take(next_p)
    win_sq[2] = square_cols(win_p[2])
    couple = [dot_full(top_inv[v], gram[v, :half, half:]) for v in range(levels + 1)]
    schur = jnp.stack([
        gram[v, half:, half:] - dot_full(gram[v, half:, :half], couple[v])
        for v in range(levels + 1)
    ])
    pass_on(first_w[1], next_w[1])
    pass_on(first_w[2], next_w[2])
    low_inv = sweep_inverse(schur, beside_low)
    pass_on(first_w[3], next_w[3])
    pass_on(first_w[4], next_w[4])
    for v in range(levels + 1):
        cross = dot_full(couple[v], low_inv[v])
        corner = top_inv[v] + dot_full(cross, couple[v], ((1,), (1,)))
        whole = jnp.concatenate([
            jnp.concatenate([corner, -cross], axis=1),
            jnp.concatenate([-cross.T, low_inv[v]], axis=1),
        ], axis=0)
        inv_high[v], inv_low[v] = split(whole)

    per = CHUNK // PIECE
    passed = 5
    for c in range(n_ch):
        span = slice(c * CHUNK, (c + 1) * CHUNK)
        while passed < n_piece and passed < max((c + 1) * per, 6 + c):
            pass_on(first_w[passed], next_w[passed])
            passed += 1

        @pl.loop(0, clusters)
        def _(k):
            cols = pl.ds(pl.multiple_of(k * pts_cl, pts_cl), pts_cl)
            out[span, cols] -= dot(window[0, span, :], tiles[1, :, cols])

    def exchange(c, level):
        at = c * levels + level
        return remote(
            sent_r.at[at], got_r.at[at], ts.at[at], tr.at[at], (clus, siblings[level][1])
        )

    def climb(c, level, node_res):
        solved = dot_split(node_res, inv_high[level], inv_low[level])
        solved_buf[c * levels + level] = solved
        sent_r[c * levels + level] = node_shift * solved[:, :half]
        exchange(c, level).start()

    def joined(c, level):
        exchange(c, level).wait()
        mine, other = sent_r[c * levels + level], got_r[c * levels + level]
        upper = siblings[level][0]
        return jnp.concatenate(
            [jnp.where(upper, other, mine), jnp.where(upper, mine, other)], axis=1
        )

    def near_stage(c):
        span = slice(c * CHUNK, (c + 1) * CHUNK)
        for i in range(c * per, (c + 1) * per):
            take(next_w[i])
        node_r[...] = jnp.zeros_like(node_r)

        @pl.loop(0, clusters)
        def _(k):
            cols = pl.ds(pl.multiple_of(k * pts_cl, pts_cl), pts_cl)
            residual = out[span, cols] - dot(window[1, span, :], tiles[2, :, cols])
            out[span, cols] = residual
            high, low = split(residual)
            node_r[...] += dot(high, pick[cols, :]) + dot(low, pick[cols, :])
        climb(c, 0, node_r[...])

    def last_stage(c):
        span = slice(c * CHUNK, (c + 1) * CHUNK)
        correction = dot_split(joined(c, levels - 1), inv_high[levels], inv_low[levels])
        for level in reversed(range(levels)):
            upper = siblings[level][0]
            inject = jnp.where(upper, correction[:, half:], correction[:, :half])
            correction = solved_buf[c * levels + level] + jnp.concatenate(
                [inject, jnp.zeros_like(inject)], axis=1
            )
        high, low = split(correction)

        @pl.loop(0, clusters)
        def _(k):
            cols = pl.ds(pl.multiple_of(k * pts_cl, pts_cl), pts_cl)
            placed = lax.dot_general(
                jnp.concatenate([high, low], axis=0), pick[cols, :], (((1,), (1,)), ((), ())),
                preferred_element_type=F32,
            )
            out[span, cols] = (
                out[span, cols] * (1.0 / (1.0 + ridge_term)) + dot(high, prolong[:, cols])
                + (placed[:CHUNK] + placed[CHUNK:])
            )

    for step in range(n_ch + levels):
        for stage in reversed(range(levels + 1)):
            c = step - stage
            if not 0 <= c < n_ch:
                continue
            if stage == 0:
                near_stage(c)
            elif stage < levels:
                climb(c, stage, joined(c, stage - 1))
            else:
                last_stage(c)

    first_p.wait_send()
    for i in range(n_piece):
        first_w[i].wait_send()

    @pl.when(has_onward)
    def _():
        next_p.wait_send()
        for i in range(n_piece):
            next_w[i].wait_send()


def on_device(n_clus, n_leaf, points, weights, targets, near_lists, tile_counts, skeleton):
    rhs, pts = weights.shape
    features = points.shape[0]
    clusters = near_lists.shape[0]
    n_skel = skeleton.shape[1]
    half = n_skel // 2
    levels = n_leaf.bit_length() - 1
    n_piece, n_ch = rhs // PIECE, rhs // CHUNK
    vmem = pl.BlockSpec(memory_space=pltpu.VMEM)
    dma = pltpu.SemaphoreType.DMA
    return pl.pallas_call(
        functools.partial(fused_kernel, n_clus, n_leaf),
        out_shape=jax.ShapeDtypeStruct((rhs, pts), F32),
        in_specs=[vmem] * 6,
        out_specs=vmem,
        scratch_shapes=[
            pltpu.VMEM((3 * clusters, pts), F32),
            pltpu.VMEM((2, rhs, pts), BF16),
            pltpu.VMEM((3, features, pts), BF16),
            pltpu.VMEM((3, pts, 128), F32),
            pltpu.VMEM((3, pts, pts), BF16),
            pltpu.VMEM((pts, n_skel), BF16),
            pltpu.VMEM((n_skel, pts), BF16),
            pltpu.VMEM((levels + 1, n_skel, n_skel), F32),
            pltpu.VMEM((levels + 1, n_skel, n_skel), BF16),
            pltpu.VMEM((levels + 1, n_skel, n_skel), BF16),
            pltpu.VMEM((levels + 1, features, n_skel), BF16),
            pltpu.VMEM((levels, features, half), BF16),
            pltpu.VMEM((CHUNK, n_skel), F32),
            pltpu.VMEM((n_ch * levels, CHUNK, half), F32),
            pltpu.VMEM((n_ch * levels, CHUNK, half), F32),
            pltpu.VMEM((n_ch * levels, CHUNK, n_skel), F32),
            dma((2,)), dma((2,)),
            dma((n_piece,)), dma((n_piece,)), dma((n_piece,)), dma((n_piece,)),
            dma((levels,)), dma((levels,)),
            dma((n_ch * levels,)), dma((n_ch * levels,)),
        ],
        compiler_params=pltpu.CompilerParams(
            collective_id=0, has_side_effects=True, vmem_limit_bytes=60 * 1024 * 1024
        ),
    )(points, weights, targets, near_lists, tile_counts.reshape(1, -1), skeleton)


def solution(mesh):
    placed = (
        P(None, ("clus", "leaf")),
        P(None, ("clus", "leaf")),
        P(None, ("clus", "leaf")),
        P(("clus", "leaf"), None),
        P(("clus", "leaf")),
        P(("clus", "leaf"), None),
    )
    return jax.shard_map(
        functools.partial(on_device, mesh.shape["clus"], mesh.shape["leaf"]),
        mesh=mesh, in_specs=placed, out_specs=P(None, ("clus", "leaf")), check_vma=False,
    )
```

```python
import functools

import jax
import jax.numpy as jnp
from jax import lax
from jax.experimental import pallas as pl
from jax.experimental.pallas import tpu as pltpu
from jax.sharding import PartitionSpec as P

ridge_term = 0.5
node_shift = 4.0
MESH = pl.DeviceIdType.MESH
F32 = jnp.float32
BF16 = jnp.bfloat16
SWEEP = 8
LOG2E = 1.4426950408889634
PIECE = 64
CHUNK = 128


def dot(a, b):
    return jnp.dot(a, b, preferred_element_type=F32)


def dot_full(a, b, dims=((1,), (0,))):
    return lax.dot_general(
        a, b, (dims, ((), ())), precision=lax.Precision.HIGHEST, preferred_element_type=F32
    )


def split(a):
    high = a.astype(BF16)
    return high, (a - high.astype(F32)).astype(BF16)


def dot_split(a, b_high, b_low):
    a_high, a_low = split(a)
    return dot(a_high, b_high) + dot(a_low, b_high) + dot(a_high, b_low)


def square_cols(pts):
    wide = pts.astype(F32)
    return dot_full(wide * wide, jnp.ones((pts.shape[0], 128), F32), ((0,), (0,)))


def square_rows(pts):
    wide = pts.astype(F32)
    return jnp.sum(wide * wide, axis=0, keepdims=True)


def kernel_tile(row_pts, row_sq, col_pts, col_sq, bias=0.0):
    scale = 2.0 / row_pts.shape[0] * LOG2E
    cross = lax.dot_general(
        row_pts, col_pts, (((0,), (0,)), ((), ())), preferred_element_type=F32
    )
    row_wide = jnp.concatenate([row_sq * -scale] * (col_pts.shape[1] // 128), axis=1)
    return jnp.exp2(cross * (2.0 * scale) + (row_wide + (col_sq * -scale + bias)))


def sweep_inverse(mats, beside):
    count, size = mats.shape[0], mats.shape[1]
    row_id = lax.broadcasted_iota(jnp.int32, (count, SWEEP, 1), 1)
    col_id = lax.broadcasted_iota(jnp.int32, (count, 1, size), 2)

    def group(step, a):
        beside(step)
        panel = a[:, :SWEEP, :]
        for i in range(0, SWEEP, 2):
            row0, row1 = panel[:, i : i + 1, :], panel[:, i + 1 : i + 2, :]
            col0, col1 = panel[:, :, i : i + 1], panel[:, :, i + 1 : i + 2]
            p00, p01, p11 = row0[:, :, i : i + 1], row0[:, :, i + 1 : i + 2], row1[:, :, i + 1 : i + 2]
            inv = 1.0 / (p00 * p11 - p01 * p01)
            i00, i01, i11 = p11 * inv, -p01 * inv, p00 * inv
            new0 = i00 * row0 + i01 * row1
            new1 = i01 * row0 + i11 * row1
            new0 = jnp.where(col_id == i, -i00, jnp.where(col_id == i + 1, -i01, new0))
            new1 = jnp.where(col_id == i, -i01, jnp.where(col_id == i + 1, -i11, new1))
            row_in = (row_id == i) | (row_id == i + 1)
            col_in = (col_id == i) | (col_id == i + 1)
            col0 = jnp.where(row_in, jnp.where(row_id == i, -1.0, 0.0), col0)
            col1 = jnp.where(row_in, jnp.where(row_id == i, 0.0, -1.0), col1)
            panel = jnp.where(row_in | col_in, 0.0, panel) - col0 * new0 - col1 * new1
        below = a[:, SWEEP:, :]
        rest = jnp.where(col_id < SWEEP, 0.0, below)
        for i in range(SWEEP):
            rest = rest - below[:, :, i : i + 1] * panel[:, i : i + 1, :]
        return pltpu.roll(jnp.concatenate([rest, panel], axis=1), size - SWEEP, 2)

    return -lax.fori_loop(0, size // SWEEP, group, mats)


def fused_kernel(
    n_clus, n_leaf,
    points, weights, targets, near_lists, tile_counts, skeleton,
    out,
    bias, window, win_p, win_sq, tiles, pick, prolong, gram, inv_high, inv_low, node_p, got_p,
    node_r, got_r, sent_r, solved_buf,
    ps, pr, as_, ar, bs, br, qs, qr, ts, tr,
):
    clus, leaf = lax.axis_index("clus"), lax.axis_index("leaf")
    levels = n_leaf.bit_length() - 1
    clusters, slots = near_lists.shape
    pts_cl = points.shape[1] // clusters
    n_skel = skeleton.shape[1]
    half = n_skel // 2
    n_piece = weights.shape[0] // PIECE
    n_ch = weights.shape[0] // CHUNK
    even = lax.rem(clus, 2) == 0
    partner = jnp.where(even, clus + 1, clus - 1)
    onward = jnp.where(even, clus + 2, clus - 2)
    behind = jnp.where(even, clus - 2, clus + 2)
    has_onward = (onward >= 0) & (onward < n_clus)
    has_behind = (behind >= 0) & (behind < n_clus)
    siblings = []
    for level in range(levels):
        upper = lax.rem(leaf // (1 << level), 2) == 1
        siblings.append((upper, jnp.where(upper, leaf - (1 << level), leaf + (1 << level))))

    barrier = pltpu.get_barrier_semaphore()
    pl.semaphore_signal(barrier, inc=1, device_id=(partner, leaf), device_id_type=MESH)
    for _, sibling in siblings:
        pl.semaphore_signal(barrier, inc=1, device_id=(clus, sibling), device_id_type=MESH)

    @pl.when(has_onward)
    def _():
        pl.semaphore_signal(barrier, inc=1, device_id=(onward, leaf), device_id_type=MESH)

    @pl.when(has_behind)
    def _():
        pl.semaphore_signal(barrier, inc=1, device_id=(behind, leaf), device_id_type=MESH)

    pl.semaphore_wait(
        barrier, 1 + levels + has_onward.astype(jnp.int32) + has_behind.astype(jnp.int32)
    )

    def remote(src, dst, send, recv, where):
        return pltpu.make_async_remote_copy(
            src_ref=src, dst_ref=dst, send_sem=send, recv_sem=recv, device_id=where,
            device_id_type=MESH,
        )

    first_p = remote(points, win_p.at[1], ps.at[0], pr.at[0], (partner, leaf))
    next_p = remote(win_p.at[1], win_p.at[2], ps.at[1], pr.at[1], (onward, leaf))
    first_p.start()
    first_w, next_w = [], []
    for i in range(n_piece):
        rows = pl.ds(i * PIECE, PIECE)
        first_w.append(remote(
            weights.at[rows], window.at[0, rows], as_.at[i], ar.at[i], (partner, leaf)
        ))
        next_w.append(remote(
            window.at[0, rows], window.at[1, rows], bs.at[i], br.at[i], (onward, leaf)
        ))
        first_w[i].start()

    def pass_on(first, after):
        first.wait_recv()

        @pl.when(has_onward)
        def _():
            after.start()

    @pl.when(jnp.logical_not(has_behind))
    def _():
        win_p[2] = jnp.zeros(points.shape, BF16)
        window[1] = jnp.zeros(weights.shape, BF16)

    def take(after):
        @pl.when(has_behind)
        def _():
            after.wait_recv()

    spot = lax.broadcasted_iota(jnp.int32, (3 * clusters, 1), 0)
    place_clus = jnp.where(
        spot < clusters, clus,
        jnp.where(spot < 2 * clusters, partner, jnp.where(even, clus - 1, clus + 1)),
    )
    spot_id = (place_clus * n_leaf + leaf) * clusters + lax.rem(spot, clusters)
    spot_id = jnp.where((place_clus >= 0) & (place_clus < n_clus), spot_id, -1)
    for k in range(clusters):
        miss = jnp.full((3 * clusters, 1), -1e30, F32)
        for s in range(slots):
            hit = (spot_id == near_lists[k : k + 1, s : s + 1]) & (s < tile_counts[:, k : k + 1])
            miss = jnp.where(hit, 0.0, miss)
        bias[:, k * pts_cl : (k + 1) * pts_cl] = jnp.broadcast_to(miss, (3 * clusters, pts_cl))

    skel = skeleton[...]
    pick[...] = (
        lax.broadcasted_iota(jnp.int32, (points.shape[1], n_skel), 0) == skel
    ).astype(BF16)
    base_p = dot(points[...], pick[...]).astype(BF16)
    node_p[0] = base_p
    own_sq_cols = square_cols(base_p)
    own_sq = square_rows(points[...])

    def build_prolong(k):
        cols = slice(k * pts_cl, (k + 1) * pts_cl)
        prolong[:, cols] = kernel_tile(
            base_p, own_sq_cols, points[:, cols], own_sq[:, cols]
        ).astype(BF16)

    for level, (upper, sibling) in enumerate(siblings):
        copy = remote(
            node_p.at[level, :, pl.ds(0, half)], got_p.at[level], qs.at[level], qr.at[level],
            (clus, sibling),
        )
        copy.start()
        if level < clusters - 1:
            build_prolong(level)
        copy.wait()
        mine, other = node_p[level, :, :half], got_p[level]
        node_p[level + 1, :, :half] = jnp.where(upper, other, mine)
        node_p[level + 1, :, half:] = jnp.where(upper, mine, other)

    for k in range(min(levels, clusters - 1), clusters):
        build_prolong(k)
    pass_on(first_p, next_p)
    win_p[0] = points[...]
    for level in range(levels + 1):
        p = node_p[level]
        shift_mat = jnp.where(
            lax.broadcasted_iota(jnp.int32, (n_skel, n_skel), 0)
            == lax.broadcasted_iota(jnp.int32, (n_skel, n_skel), 1),
            node_shift, 0.0,
        )
        gram[level] = kernel_tile(p, square_cols(p), p, square_rows(p)) + shift_mat

    def build(place, r):
        rows = pl.ds(pl.multiple_of(r * 128, 128), 128)
        q = pl.ds(place * clusters + r * 128 // pts_cl, 1)
        for k in range(clusters):
            cols = slice(k * pts_cl, (k + 1) * pts_cl)
            tiles[place, rows, cols] = kernel_tile(
                win_p[place, :, rows], win_sq[place, rows, :],
                points[:, cols], own_sq[:, cols], bias[q, cols],
            ).astype(BF16)

    n_block = points.shape[1] // 128
    n_step = half // SWEEP
    per_step = -(-n_block // n_step)

    def beside_top(step):
        for t in range(per_step):
            build(0, step * per_step + t)
            build(1, step * per_step + t)

    own_rows = weights.shape[0] * clusters // n_step

    def beside_low(step):
        for t in range(per_step):
            build(2, step * per_step + t)
        span = pl.ds(pl.multiple_of(step // clusters * own_rows, own_rows), own_rows)
        cols = pl.ds(pl.multiple_of(lax.rem(step, clusters) * pts_cl, pts_cl), pts_cl)
        out[span, cols] = (
            targets[span, cols].astype(F32) - ridge_term * weights[span, cols].astype(F32)
            - dot(weights[span, :], tiles[0, :, cols])
        )

    win_sq[0] = square_cols(win_p[0])
    win_sq[1] = square_cols(win_p[1])
    top_inv = sweep_inverse(gram[:, :half, :half], beside_top)
    pass_on(first_w[0], next_w[0])
    take(next_p)
    win_sq[2] = square_cols(win_p[2])
    couple = [dot_full(top_inv[v], gram[v, :half, half:]) for v in range(levels + 1)]
    schur = jnp.stack([
        gram[v, half:, half:] - dot_full(gram[v, half:, :half], couple[v])
        for v in range(levels + 1)
    ])
    pass_on(first_w[1], next_w[1])
    pass_on(first_w[2], next_w[2])
    low_inv = sweep_inverse(schur, beside_low)
    pass_on(first_w[3], next_w[3])
    pass_on(first_w[4], next_w[4])
    for v in range(levels + 1):
        cross = dot_full(couple[v], low_inv[v])
        corner = top_inv[v] + dot_full(cross, couple[v], ((1,), (1,)))
        whole = jnp.concatenate([
            jnp.concatenate([corner, -cross], axis=1),
            jnp.concatenate([-cross.T, low_inv[v]], axis=1),
        ], axis=0)
        inv_high[v], inv_low[v] = split(whole)

    per = CHUNK // PIECE
    passed = 5
    for c in range(n_ch):
        span = slice(c * CHUNK, (c + 1) * CHUNK)
        while passed < n_piece and passed < max((c + 1) * per, 6 + c):
            pass_on(first_w[passed], next_w[passed])
            passed += 1

        @pl.loop(0, clusters)
        def _(k):
            cols = pl.ds(pl.multiple_of(k * pts_cl, pts_cl), pts_cl)
            out[span, cols] -= dot(window[0, span, :], tiles[1, :, cols])

    def exchange(c, level):
        at = c * levels + level
        return remote(
            sent_r.at[at], got_r.at[at], ts.at[at], tr.at[at], (clus, siblings[level][1])
        )

    def climb(c, level, node_res):
        solved = dot_split(node_res, inv_high[level], inv_low[level])
        solved_buf[c * levels + level] = solved
        sent_r[c * levels + level] = node_shift * solved[:, :half]
        exchange(c, level).start()

    def joined(c, level):
        exchange(c, level).wait()
        mine, other = sent_r[c * levels + level], got_r[c * levels + level]
        upper = siblings[level][0]
        return jnp.concatenate(
            [jnp.where(upper, other, mine), jnp.where(upper, mine, other)], axis=1
        )

    def near_stage(c):
        span = slice(c * CHUNK, (c + 1) * CHUNK)
        for i in range(c * per, (c + 1) * per):
            take(next_w[i])
        node_r[...] = jnp.zeros_like(node_r)

        @pl.loop(0, clusters)
        def _(k):
            cols = pl.ds(pl.multiple_of(k * pts_cl, pts_cl), pts_cl)
            residual = out[span, cols] - dot(window[1, span, :], tiles[2, :, cols])
            out[span, cols] = residual
            high, low = split(residual)
            node_r[...] += dot(high, pick[cols, :]) + dot(low, pick[cols, :])
        climb(c, 0, node_r[...])

    def last_stage(c):
        span = slice(c * CHUNK, (c + 1) * CHUNK)
        correction = dot_split(joined(c, levels - 1), inv_high[levels], inv_low[levels])
        for level in reversed(range(levels)):
            upper = siblings[level][0]
            inject = jnp.where(upper, correction[:, half:], correction[:, :half])
            correction = solved_buf[c * levels + level] + jnp.concatenate(
                [inject, jnp.zeros_like(inject)], axis=1
            )
        high, low = split(correction)

        @pl.loop(0, clusters)
        def _(k):
            cols = pl.ds(pl.multiple_of(k * pts_cl, pts_cl), pts_cl)
            placed = lax.dot_general(
                jnp.concatenate([high, low], axis=0), pick[cols, :], (((1,), (1,)), ((), ())),
                preferred_element_type=F32,
            )
            out[span, cols] = (
                out[span, cols] * (1.0 / (1.0 + ridge_term)) + dot(high, prolong[:, cols])
                + (placed[:CHUNK] + placed[CHUNK:])
            )

    for step in range(n_ch + levels):
        for stage in reversed(range(levels + 1)):
            c = step - stage
            if not 0 <= c < n_ch:
                continue
            if stage == 0:
                near_stage(c)
            elif stage < levels:
                climb(c, stage, joined(c, stage - 1))
            else:
                last_stage(c)

    first_p.wait_send()
    for i in range(n_piece):
        first_w[i].wait_send()

    @pl.when(has_onward)
    def _():
        next_p.wait_send()
        for i in range(n_piece):
            next_w[i].wait_send()


def on_device(n_clus, n_leaf, points, weights, targets, near_lists, tile_counts, skeleton):
    rhs, pts = weights.shape
    features = points.shape[0]
    clusters = near_lists.shape[0]
    n_skel = skeleton.shape[1]
    half = n_skel // 2
    levels = n_leaf.bit_length() - 1
    n_piece, n_ch = rhs // PIECE, rhs // CHUNK
    vmem = pl.BlockSpec(memory_space=pltpu.VMEM)
    dma = pltpu.SemaphoreType.DMA
    return pl.pallas_call(
        functools.partial(fused_kernel, n_clus, n_leaf),
        out_shape=jax.ShapeDtypeStruct((rhs, pts), F32),
        in_specs=[vmem] * 6,
        out_specs=vmem,
        scratch_shapes=[
            pltpu.VMEM((3 * clusters, pts), F32),
            pltpu.VMEM((2, rhs, pts), BF16),
            pltpu.VMEM((3, features, pts), BF16),
            pltpu.VMEM((3, pts, 128), F32),
            pltpu.VMEM((3, pts, pts), BF16),
            pltpu.VMEM((pts, n_skel), BF16),
            pltpu.VMEM((n_skel, pts), BF16),
            pltpu.VMEM((levels + 1, n_skel, n_skel), F32),
            pltpu.VMEM((levels + 1, n_skel, n_skel), BF16),
            pltpu.VMEM((levels + 1, n_skel, n_skel), BF16),
            pltpu.VMEM((levels + 1, features, n_skel), BF16),
            pltpu.VMEM((levels, features, half), BF16),
            pltpu.VMEM((CHUNK, n_skel), F32),
            pltpu.VMEM((n_ch * levels, CHUNK, half), F32),
            pltpu.VMEM((n_ch * levels, CHUNK, half), F32),
            pltpu.VMEM((n_ch * levels, CHUNK, n_skel), F32),
            dma((2,)), dma((2,)),
            dma((n_piece,)), dma((n_piece,)), dma((n_piece,)), dma((n_piece,)),
            dma((levels,)), dma((levels,)),
            dma((n_ch * levels,)), dma((n_ch * levels,)),
        ],
        compiler_params=pltpu.CompilerParams(
            collective_id=0, has_side_effects=True, vmem_limit_bytes=60 * 1024 * 1024
        ),
    )(points, weights, targets, near_lists, tile_counts.reshape(1, -1), skeleton)


def solution(mesh):
    placed = (
        P(None, ("clus", "leaf")),
        P(None, ("clus", "leaf")),
        P(None, ("clus", "leaf")),
        P(("clus", "leaf"), None),
        P(("clus", "leaf")),
        P(("clus", "leaf"), None),
    )
    return jax.shard_map(
        functools.partial(on_device, mesh.shape["clus"], mesh.shape["leaf"]),
        mesh=mesh, in_specs=placed, out_specs=P(None, ("clus", "leaf")), check_vma=False,
    )
```
